512 devices in a mesh: dp: 32 (over z, core), tp: 16 (over x, y).
Axes of the slice: x: 4, y: 4, z: 16, core: 2. Of those that a mesh axis runs over, the one named last changes fastest.
Arguments:
- tokens: bfloat16 [16384, 2048], P(('dp', 'tp')), may hold values from -6 to 6
- norm_gain: float32 [2048], replicated, may hold values from 0.5 to 1.5
- w_query: bfloat16 [2048, 2048], P('dp', 'tp'), may hold values from -0.125 to 0.125
- w_key: bfloat16 [2048, 2048], P('dp', 'tp'), may hold values from -0.125 to 0.125
- w_value: bfloat16 [2048, 4096], P('dp', 'tp'), may hold values from -0.125 to 0.125
- w_gate: bfloat16 [2048, 4096], P('dp', 'tp'), may hold values from -0.125 to 0.125
- w_beta: bfloat16 [2048, 32], P('dp', 'tp'), may hold values from -0.125 to 0.125
- w_decay: bfloat16 [2048, 32], P('dp', 'tp'), may hold values from -0.125 to 0.125
- conv_query: float32 [4, 2048], P(None, 'tp'), may hold values from -3 to 3
- conv_key: float32 [4, 2048], P(None, 'tp'), may hold values from -3 to 3
- conv_value: float32 [4, 4096], P(None, 'tp'), may hold values from -3 to 3
- decay_rate: float32 [32], P('tp'), may hold values from 0.004 to 0.04
- dt_bias: float32 [32], P('tp'), may hold values from -1 to 1
- out_gain: float32 [128], replicated, may hold values from 0.5 to 1.5
- seg_ids: int32 [32, 512], P('dp'), may hold values from 0 to 15, never falling along the last dimension, each value on 1 to 128 neighbouring positions
Outputs:
- mixed_tiles: bfloat16 [16384, 4096], P(('dp', 'tp'))
The draws below stay inside these ranges and needn't reach their ends.
Inputs may be any that keep to these rules, and one draw needn't show every extreme that they name: Each row of seg_ids never falls; every prompt covers 1 to 128 consecutive positions.
All inputs are finite; a program needn't handle non-finite values.
Results may differ from the reference program's by a relative error of at most 0.0034.
The reference program's roundings to bfloat16 on the way (of `normed`) count: a program that leaves them out, or rounds other values in their place, can miss the bound.
Values may be sent and summed in bfloat16 or wider, within the bound.
No kernel may reach another device: no remote copies, remote signals or barrier semaphores. Data moves between devices by JAX's collectives and lax.ppermute only.
A program may use at most 64 MiB of HBM per device.

```python
import math
import jax
import jax.numpy as jnp
import numpy as np
from jax import lax

D = 2048
KH = 16
VH = 32
DK = 128
DV = 128
CONV_K = 4
SPAN = 64
SEGS = 16
ROWS = 512
TOKENS = 16384
N_DP = 32


def shard_levels(key, extent, cuts, low, high):
    def one(axis_at, blocks):
        draws = jax.random.uniform(jax.random.fold_in(jax.random.fold_in(key, 6), axis_at), (blocks,), jnp.float32, low / len(cuts), high / len(cuts))
        return jnp.repeat(jnp.exp(draws), extent[axis_at] // blocks).reshape((-1,) + (1,) * (len(extent) - axis_at - 1))

    level = one(*cuts[0])
    for cut in cuts[1:]:
        level = level * one(*cut)
    return level


def profile(amount, total, most, lean):
    portions = [(1 << 20) // math.isqrt(grade ** lean) + 1 for grade in range(2, amount + 1)]
    spare, given = total - most - (amount - 1), [1] * (amount - 1)
    while spare > 0:
        candidates = [i for i in range(amount - 1) if given[i] < most]
        pool, budget = sum([portions[i] for i in candidates]), spare
        for i in candidates:
            addition = min(most - given[i], max(1, budget * portions[i] // pool), spare)
            given[i] = given[i] + addition
            spare = spare - addition
    return np.array([most] + given)


def uneven(rng, number_of, total, most, slope):
    if number_of == 2:
        one = jax.random.randint(rng, (), max(1, total - most), min(most, total - 1) + 1)
        return jnp.stack([one, total - one])
    lengths = jnp.asarray(profile(number_of, total, most, slope), jnp.int32)
    couples = (number_of - 1) // 2
    donor, taker = lengths[1:1 + 2 * couples:2], lengths[2:2 + 2 * couples:2]
    slack = jnp.minimum(donor - 1, most - taker)
    moved = jax.random.randint(jax.random.fold_in(rng, 1), (couples,), 0, 1 << 20) % (slack + 1)
    lengths = lengths.at[1:1 + 2 * couples:2].set(donor - moved).at[2:2 + 2 * couples:2].set(taker + moved)
    return lengths[jax.random.permutation(jax.random.fold_in(rng, 2), number_of)]


def normal_values(own_key, dims, deviation, limit, cuts=(), kind=jnp.bfloat16):
    loudness = shard_levels(own_key, dims, cuts, -0.22, 0.18) if cuts else 1.0
    array = jax.random.normal(own_key, dims, jnp.float32) * deviation * loudness
    return jnp.minimum(jnp.maximum(array, -limit), limit).astype(kind)


def setup_inputs(seed: int = 0) -> dict:
    streams_of = jax.random.split(jax.random.key(seed), 16)
    tokens = normal_values(streams_of[0], (TOKENS, D), 1.0, 6.0, ((0, 512),))
    norm_gain = jnp.clip(1.0 + 0.1 * jax.random.normal(streams_of[1], (D,), jnp.float32), 0.5, 1.5)
    w_query = normal_values(streams_of[2], (D, KH * DK), D ** -0.5, 0.125, ((0, 32), (1, 16)))
    w_key = normal_values(streams_of[3], (D, KH * DK), D ** -0.5, 0.125, ((0, 32), (1, 16)))
    w_value = normal_values(streams_of[4], (D, VH * DV), D ** -0.5, 0.125, ((0, 32), (1, 16)))
    w_gate = normal_values(streams_of[5], (D, VH * DV), D ** -0.5, 0.125, ((0, 32), (1, 16)))
    w_beta = normal_values(streams_of[6], (D, VH), D ** -0.5, 0.125, ((0, 32), (1, 16)))
    w_decay = normal_values(streams_of[7], (D, VH), D ** -0.5, 0.125, ((0, 32), (1, 16)))
    conv_query = normal_values(streams_of[8], (CONV_K, KH * DK), 0.5, 3.0, ((1, 16),), jnp.float32)
    conv_key = normal_values(streams_of[9], (CONV_K, KH * DK), 0.5, 3.0, ((1, 16),), jnp.float32)
    conv_value = normal_values(streams_of[10], (CONV_K, VH * DV), 0.5, 3.0, ((1, 16),), jnp.float32)
    decay_rate = jnp.clip(jnp.exp(math.log(0.04) - 2.30258502 * jax.random.uniform(streams_of[11], (VH,), jnp.float32) ** shard_levels(streams_of[11], (VH,), ((0, 16),), -0.2, 0.2)), 0.004, 0.04)
    dt_bias = jnp.clip(jax.random.uniform(streams_of[12], (VH,), jnp.float32, -1.0, 1.0) * shard_levels(streams_of[12], (VH,), ((0, 16),), -0.4, 0.0), -1.0, 1.0)
    out_gain = jnp.clip(1.0 + 0.1 * jax.random.normal(streams_of[13], (DV,), jnp.float32), 0.5, 1.5)
    seg_ids = jax.vmap(lambda own: jnp.searchsorted(jnp.cumsum(uneven(own, SEGS, ROWS, ROWS // 4, 2)), jnp.arange(ROWS), side="right"))(jax.random.split(streams_of[14], N_DP)).reshape((N_DP, ROWS)).astype(jnp.int32)
    return {"tokens": tokens, "norm_gain": norm_gain, "w_query": w_query, "w_key": w_key, "w_value": w_value, "w_gate": w_gate, "w_beta": w_beta, "w_decay": w_decay, "conv_query": conv_query, "conv_key": conv_key, "conv_value": conv_value, "decay_rate": decay_rate, "dt_bias": dt_bias, "out_gain": out_gain, "seg_ids": seg_ids}


highest = lax.Precision.HIGHEST

def rms_rows(tokens, gain):
    floats = tokens.astype(jnp.float32)
    scaled = floats * lax.rsqrt(lax.optimization_barrier(jnp.mean(floats * floats, axis=-1, keepdims=True)) + 1e-06)
    return (scaled * gain).astype(jnp.bfloat16)

def split_columns(projected, column_counts):
    pieces = []
    offset = 0
    for count in column_counts:
        pieces.append(projected[:, offset:offset + count])
        offset = offset + count
    return pieces

def causal_conv(projected, kernel, segment):
    kernel_len = kernel.shape[0]
    summed = projected * kernel[kernel_len - 1]
    for offset in range(1, kernel_len):
        zeros_top = jnp.zeros((offset, projected.shape[1]), jnp.float32)
        shifted = jnp.concatenate([zeros_top, projected[:-offset]], axis=0)
        earlier = jnp.concatenate([jnp.full((offset,), -1, jnp.int32), segment[:-offset]])
        same_doc = (earlier == segment).astype(jnp.float32)
        summed = summed + shifted * same_doc[:, None] * kernel[kernel_len - 1 - offset]
    return jax.nn.silu(summed)

def unit_heads(values, heads, head_size):
    shaped = values.reshape(values.shape[0], heads, head_size)
    return shaped * lax.rsqrt(lax.optimization_barrier(jnp.sum(shaped * shaped, axis=-1, keepdims=True)) + 1e-06)

def delta_head(query, key_rows, value, beta, log_decay, segment):
    row_count = query.shape[0]
    blocks = row_count // SPAN
    value_size = value.shape[1]
    q_blocks = query.reshape(blocks, SPAN, query.shape[1])
    k_blocks = key_rows.reshape(blocks, SPAN, key_rows.shape[1])
    v_blocks = value.reshape(blocks, SPAN, value_size)
    beta_blocks = beta.reshape(blocks, SPAN)
    decay_blocks = log_decay.reshape(blocks, SPAN)
    seg_blocks = segment.reshape(blocks, SPAN)
    before = jnp.concatenate([jnp.full((1,), -1, jnp.int32), seg_blocks[:-1, -1]])
    row_index = lax.broadcasted_iota(jnp.int32, (SPAN, SPAN), 0)
    col_index = lax.broadcasted_iota(jnp.int32, (SPAN, SPAN), 1)
    lower_mask = row_index >= col_index
    strict = row_index > col_index

    def advance(state, inputs):
        block_q, block_k, block_v, block_beta, block_decay, block_seg, block_before = inputs
        cumulative = jnp.cumsum(block_decay)
        same_doc = block_seg[:, None] == block_seg[None, :]
        spread = jnp.where(lower_mask, cumulative[:, None] - cumulative[None, :], 0.0)
        decay_matrix = jnp.where(lower_mask & same_doc, jnp.exp(spread), 0.0)
        carried = (block_seg == block_before).astype(jnp.float32)
        from_start = jnp.exp(cumulative) * carried
        key_gram = jnp.dot(block_k, block_k.T, precision=highest)
        lower_matrix = jnp.where(strict, block_beta[:, None] * key_gram * decay_matrix, 0.0)
        system = jnp.eye(SPAN, dtype=jnp.float32) + lower_matrix
        right_side = jnp.concatenate([block_beta[:, None] * block_v, (block_beta * from_start)[:, None] * block_k], axis=1)
        solved = lax.linalg.triangular_solve(system, right_side, left_side=True, lower=True, unit_diagonal=True)
        updates = solved[:, :value_size] - jnp.dot(solved[:, value_size:], state, precision=highest)
        scores = jnp.dot(block_q, block_k.T, precision=highest) * decay_matrix
        output = jnp.dot(from_start[:, None] * block_q, state, precision=highest) + jnp.dot(scores, updates, precision=highest)
        tail_weight = jnp.where(block_seg == block_seg[-1], jnp.exp(cumulative[-1] - cumulative), 0.0)
        new_state = jnp.exp(cumulative[-1]) * carried[-1] * state + jnp.dot((tail_weight[:, None] * block_k).T, updates, precision=highest)
        return (new_state, output)
    initial = jnp.zeros((key_rows.shape[1], value_size), jnp.float32)
    last_state, outputs = lax.scan(advance, initial, (q_blocks, k_blocks, v_blocks, beta_blocks, decay_blocks, seg_blocks, before))
    return outputs.reshape(row_count, value_size)

def mix_rows(parts, segment, conv_query, conv_key, conv_value, decay_rate, dt_bias, out_gain):
    proj_query, proj_key, proj_value, proj_gate, proj_beta, proj_decay = [piece_part.astype(jnp.float32) for piece_part in parts]
    key_heads = proj_query.shape[1] // DK
    value_heads = proj_value.shape[1] // DV
    repeat = value_heads // key_heads
    query = unit_heads(causal_conv(proj_query, conv_query, segment), key_heads, DK) * DK ** (-0.5)
    keys = unit_heads(causal_conv(proj_key, conv_key, segment), key_heads, DK)
    values = causal_conv(proj_value, conv_value, segment).reshape(proj_value.shape[0], value_heads, DV)
    query = jnp.repeat(query, repeat, axis=1)
    keys = jnp.repeat(keys, repeat, axis=1)
    beta = jax.nn.sigmoid(proj_beta)
    log_decay = -decay_rate * jax.nn.softplus(proj_decay + dt_bias)
    mixed = jax.vmap(delta_head, in_axes=(1, 1, 1, 1, 1, None), out_axes=1)(query, keys, values, beta, log_decay, segment)
    normed = mixed * lax.rsqrt(lax.optimization_barrier(jnp.mean(mixed * mixed, axis=-1, keepdims=True)) + 1e-06) * out_gain
    gated = normed * jax.nn.silu(proj_gate.reshape(proj_gate.shape[0], value_heads, DV))
    return gated.reshape(gated.shape[0], value_heads * DV).astype(jnp.bfloat16)

def reference(tokens, norm_gain, w_query, w_key, w_value, w_gate, w_beta, w_decay, conv_query, conv_key, conv_value, decay_rate, dt_bias, out_gain, seg_ids):
    weights = [w_query, w_key, w_value, w_gate, w_beta, w_decay]
    column_counts = [matrix.shape[1] for matrix in weights]
    joined = jnp.concatenate(weights, axis=1)
    groups = tokens.reshape(N_DP, ROWS, D)

    def one_group(operands):
        group_rows, segment = operands
        projected = jnp.dot(rms_rows(group_rows, norm_gain).astype(jnp.float32), joined.astype(jnp.float32), preferred_element_type=jnp.float32).astype(jnp.bfloat16)
        parts = split_columns(projected, column_counts)
        return mix_rows(parts, segment, conv_query, conv_key, conv_value, decay_rate, dt_bias, out_gain)
    mixed = lax.map(one_group, (groups, seg_ids))
    return mixed.reshape(TOKENS, VH * DV)
```

```python
import jax
import jax.numpy as jnp
from jax import lax
from jax.experimental import pallas as pl
from jax.experimental.pallas import tpu as pltpu
from jax.sharding import PartitionSpec as P

BLOCK = 128
BASE = 16


def split_two(x):
    high = x.astype(jnp.bfloat16)
    low = (x - high.astype(jnp.float32)).astype(jnp.bfloat16)
    return high, low


def dot_split(a, b):
    ah, al = split_two(a)
    bh, bl = split_two(b)
    return jnp.dot(
        jnp.concatenate([ah, al, ah], axis=1),
        jnp.concatenate([bh, bh, bl], axis=0),
        preferred_element_type=jnp.float32,
    )


def iota(shape, axis):
    return lax.broadcasted_iota(jnp.int32, shape, axis)


def silu(x):
    return x / (1.0 + jnp.exp(-x))


def softplus(x):
    return jnp.maximum(x, 0.0) + jnp.log1p(jnp.exp(-jnp.abs(x)))


def columns_of(rows):
    filled = jnp.concatenate(
        [rows, jnp.zeros((128 - rows.shape[0], rows.shape[1]), jnp.float32)], axis=0
    )
    return filled.T


def conv_silu(p, taps, masks):
    summed = p * taps[3:4, :]
    for offset in range(1, 4):
        shifted = pltpu.roll(p, offset, 0)
        summed = summed + shifted * masks[offset - 1] * taps[3 - offset : 4 - offset, :]
    return silu(summed)


def unit(x):
    return x * lax.rsqrt(jnp.sum(x * x, axis=-1, keepdims=True) + 1e-06)


def mix_kernel(
    rate_ref, bias_ref, x0_ref, x1_ref, x2_ref, x3_ref, w_ref, seg_ref, tq_ref, tk_ref, tv_ref, gain_ref,
    out_ref, x_ref, p_ref
):
    rows = p_ref.shape[0]
    quarter = rows // 4
    mine = lax.axis_index("tp") // 4
    for ref, behind in ((x0_ref, 0), (x1_ref, 1), (x2_ref, 2), (x3_ref, 3)):
        place = lax.rem(mine + 4 - behind, 4)
        x_ref[pl.ds(pl.multiple_of(place * quarter, quarter), quarter), :] = ref[...]
    p_ref[...] = jnp.dot(x_ref[...], w_ref[...], preferred_element_type=jnp.float32).astype(jnp.bfloat16)
    blocks = rows // BLOCK
    seg_row = seg_ref[...].astype(jnp.float32)
    position = iota((1, rows), 1)
    masks = []
    for offset in range(1, 4):
        earlier = pltpu.roll(jnp.broadcast_to(seg_row, (8, rows)), offset, 1)[0:1]
        masks.append(jnp.where((position >= offset) & (earlier == seg_row), 1.0, 0.0))

    ba = p_ref[:, 768:896].astype(jnp.float32).T
    beta = 1.0 / (1.0 + jnp.exp(-ba[0:2]))
    rate = jnp.where(iota((2, 1), 0) == 0, rate_ref[0], rate_ref[1])
    bias = jnp.where(iota((2, 1), 0) == 0, bias_ref[0], bias_ref[1])
    decay = -rate * softplus(ba[2:4] + bias)
    upper = (iota((BLOCK, BLOCK), 0) <= iota((BLOCK, BLOCK), 1)).astype(jnp.bfloat16)
    decay_wide = jnp.concatenate([decay, jnp.zeros((6, rows), jnp.float32)], axis=0)
    stacked = jnp.concatenate(
        [decay_wide[:, b * BLOCK : (b + 1) * BLOCK] for b in range(blocks)], axis=0
    )
    high, low = split_two(stacked)
    lowest = (stacked - high.astype(jnp.float32) - low.astype(jnp.float32)).astype(jnp.bfloat16)
    total = jnp.dot(
        jnp.concatenate([high, low, lowest], axis=1),
        jnp.concatenate([upper, upper, upper], axis=0),
        preferred_element_type=jnp.float32,
    )
    cumulative, start, tail = [], [], []
    for b in range(blocks):
        part = total[8 * b : 8 * b + 2]
        seg_part = seg_row[:, b * BLOCK : (b + 1) * BLOCK]
        if b == 0:
            carried = jnp.zeros((1, BLOCK), jnp.float32)
        else:
            carried = jnp.where(seg_part == seg_row[:, b * BLOCK - 1 : b * BLOCK], 1.0, 0.0)
        closing = jnp.where(seg_part == seg_part[:, BLOCK - 1 :], 1.0, 0.0)
        cumulative.append(part)
        start.append(jnp.exp(part) * carried)
        tail.append(jnp.exp(part[:, BLOCK - 1 :] - part) * closing)
    cumulative = jnp.concatenate(cumulative, axis=1)
    start = jnp.concatenate(start, axis=1)
    tail = jnp.concatenate(tail, axis=1)
    cols = columns_of(
        jnp.concatenate([beta, cumulative, start, tail, beta * start, seg_row] + masks, axis=0)
    )
    mask_cols = [cols[:, 11 + i : 12 + i] for i in range(3)]

    query = unit(conv_silu(p_ref[:, 0:128].astype(jnp.float32), tq_ref[...], mask_cols)) * 128 ** (-0.5)
    key = unit(conv_silu(p_ref[:, 128:256].astype(jnp.float32), tk_ref[...], mask_cols))
    values = [
        conv_silu(
            p_ref[:, 256 + 128 * h : 384 + 128 * h].astype(jnp.float32),
            tv_ref[:, 128 * h : 128 * (h + 1)],
            mask_cols,
        )
        for h in range(2)
    ]

    row_at = iota((BLOCK, BLOCK), 0)
    col_at = iota((BLOCK, BLOCK), 1)
    base_diagonal = (row_at // BASE) == (col_at // BASE)
    picks = jnp.concatenate(
        [((row_at // BASE == col_at // BASE) & (row_at % BASE == j)).astype(jnp.bfloat16) for j in range(BASE - 1)],
        axis=1,
    )
    picks = jnp.concatenate([picks, picks], axis=0)

    problems = [(b, h) for b in range(blocks) for h in range(2)]
    scores, lowers, packed = {}, {}, []
    for b in range(blocks):
        span = slice(b * BLOCK, (b + 1) * BLOCK)
        k_b = key[span]
        grams = dot_split(jnp.concatenate([k_b, query[span]], axis=0), k_b.T)
        same = cols[span, 10:11] == seg_row[:, span]
        for h in range(2):
            spread = jnp.where(row_at >= col_at, cols[span, 2 + h : 3 + h] - cumulative[h : h + 1, span], 0.0)
            matrix = jnp.where((row_at >= col_at) & same, jnp.exp(spread), 0.0)
            scores[b, h] = grams[BLOCK:] * matrix
            lowers[b, h] = jnp.where(
                row_at > col_at, cols[span, h : h + 1] * grams[:BLOCK] * matrix, 0.0
            )
            masked = jnp.where(base_diagonal, lowers[b, h], 0.0)
            slab = masked[0:BASE]
            for d in range(1, BLOCK // BASE):
                slab = slab + masked[d * BASE : (d + 1) * BASE]
            packed.append(slab)
    high, low = split_two(jnp.concatenate(packed, axis=0))
    spread_columns = jnp.dot(
        jnp.concatenate([high, low], axis=1), picks, preferred_element_type=jnp.float32
    )
    unit_rows = (iota((BASE, BLOCK), 0) == iota((BASE, BLOCK), 1) % BASE).astype(jnp.float32)
    inverses = []
    for i in range(len(problems)):
        solved = unit_rows
        for j in range(BASE - 1):
            factor = spread_columns[i * BASE : (i + 1) * BASE, j * BLOCK : (j + 1) * BLOCK]
            solved = solved - factor * solved[j : j + 1]
        inverses.append(solved)

    first, state = {}, {}
    for i, (b, h) in enumerate(problems):
        span = slice(b * BLOCK, (b + 1) * BLOCK)
        inverse = jnp.where(base_diagonal, jnp.concatenate([inverses[i]] * (BLOCK // BASE), axis=0), 0.0)
        size = BASE
        while size < BLOCK:
            below = (row_at // (2 * size) == col_at // (2 * size)) & (row_at // size != col_at // size)
            off = jnp.where(below, lowers[b, h], 0.0)
            inverse = inverse - dot_split(dot_split(inverse, off), inverse)
            size = 2 * size
        right = jnp.concatenate(
            [cols[span, h : h + 1] * values[h][span], cols[span, 8 + h : 9 + h] * key[span]], axis=1
        )
        solved = dot_split(inverse, right)
        first[b, h] = solved
        if b < blocks - 1:
            state[b + 1, h] = dot_split((cols[span, 6 + h : 7 + h] * key[span]).T, solved[:, :128])
    gain = gain_ref[...]
    for b, h in problems:
        span = slice(b * BLOCK, (b + 1) * BLOCK)
        update = first[b, h][:, :128]
        if b > 0:
            both = dot_split(
                jnp.concatenate([first[b, h][:, 128:], cols[span, 4 + h : 5 + h] * query[span]], axis=0),
                state[b, h],
            )
            update = update - both[:BLOCK]
            mixed = both[BLOCK:] + dot_split(scores[b, h], update)
        else:
            mixed = dot_split(scores[b, h], update)
        normed = mixed * lax.rsqrt(jnp.mean(mixed * mixed, axis=-1, keepdims=True) + 1e-06) * gain
        gate = silu(p_ref[span, 512 + 128 * h : 640 + 128 * h].astype(jnp.float32))
        out_ref[span, 128 * h : 128 * (h + 1)] = (normed * gate).astype(jnp.bfloat16)


def rms_rows(tokens, gain):
    floats = tokens.astype(jnp.float32)
    scaled = floats * lax.rsqrt(jnp.mean(floats * floats, axis=-1, keepdims=True) + 1e-06)
    return (scaled * gain).astype(jnp.bfloat16)


def shards(
    tokens,
    norm_gain,
    w_query,
    w_key,
    w_value,
    w_gate,
    w_beta,
    w_decay,
    conv_query,
    conv_key,
    conv_value,
    decay_rate,
    dt_bias,
    out_gain,
    seg_ids,
):
    joined = jnp.concatenate(
        [w_query, w_key, w_value, w_gate, w_beta, w_decay, jnp.zeros((w_beta.shape[0], 124), jnp.bfloat16)], axis=1
    )
    weights = lax.all_gather(joined, "dp", axis=0, tiled=True)
    normed = rms_rows(tokens, norm_gain)
    lines = [[4 * x + y for y in range(4)] for x in range(4)]
    quarter = lax.all_gather(normed, "tp", axis=0, tiled=True, axis_index_groups=lines)

    def from_behind(shift):
        return lax.ppermute(quarter, "tp", [(i, (i + 4 * shift) % 16) for i in range(16)])

    rows = [quarter, from_behind(1), from_behind(2), from_behind(3)]
    vmem = pl.BlockSpec(memory_space=pltpu.VMEM)
    smem = pl.BlockSpec(memory_space=pltpu.SMEM)
    tiles = pl.pallas_call(
        mix_kernel,
        out_shape=jax.ShapeDtypeStruct((512, 256), jnp.bfloat16),
        in_specs=[smem, smem] + [vmem] * 10,
        out_specs=vmem,
        scratch_shapes=[pltpu.VMEM((512, 2048), jnp.bfloat16), pltpu.VMEM((512, 896), jnp.bfloat16)],
        compiler_params=pltpu.CompilerParams(vmem_limit_bytes=40 * 1024 * 1024),
    )(decay_rate, dt_bias, *rows, weights, seg_ids, conv_query, conv_key, conv_value, out_gain.reshape(1, 128))
    return lax.all_to_all(tiles, "tp", split_axis=0, concat_axis=1, tiled=True)


def solution(mesh):
    in_specs = (
        P(("dp", "tp"), None),
        P(),
        P("dp", "tp"),
        P("dp", "tp"),
        P("dp", "tp"),
        P("dp", "tp"),
        P("dp", "tp"),
        P("dp", "tp"),
        P(None, "tp"),
        P(None, "tp"),
        P(None, "tp"),
        P("tp"),
        P("tp"),
        P(),
        P("dp", None),
    )
    out_specs = P(("dp", "tp"), None)
    return jax.shard_map(shards, mesh=mesh, in_specs=in_specs, out_specs=out_specs, check_vma=False)
```

```python
import jax
import jax.numpy as jnp
from jax import lax
from jax.experimental import pallas as pl
from jax.experimental.pallas import tpu as pltpu
from jax.sharding import PartitionSpec as P

BLOCK = 128
BASE = 16
NEAR = (0, 4, 2, 6)
FAR = (1, 5, 3, 7)


def split_two(x):
    high = x.astype(jnp.bfloat16)
    low = (x - high.astype(jnp.float32)).astype(jnp.bfloat16)
    return high, low


def dot_split(a, b):
    ah, al = split_two(a)
    bh, bl = split_two(b)
    if b.shape[1] > 128:
        high = jnp.concatenate([bh, bh], axis=0)
        both = jnp.concatenate([ah, al], axis=1)
        return jnp.dot(both, high, preferred_element_type=jnp.float32) + jnp.dot(
            ah, bl, preferred_element_type=jnp.float32
        )
    halves = jnp.concatenate([bh, bl], axis=1)
    both = jnp.dot(
        jnp.concatenate([ah, al], axis=1),
        jnp.concatenate([halves, halves], axis=0),
        preferred_element_type=jnp.float32,
    )
    return both[:, : b.shape[1]] + both[:, b.shape[1] :]


def iota(shape, axis):
    return lax.broadcasted_iota(jnp.int32, shape, axis)


def silu(x):
    return x / (1.0 + jnp.exp(-x))


def softplus(x):
    return jnp.maximum(x, 0.0) + jnp.log1p(jnp.exp(-jnp.abs(x)))


def columns_of(rows):
    filled = jnp.concatenate(
        [rows, jnp.zeros((128 - rows.shape[0], rows.shape[1]), jnp.float32)], axis=0
    )
    return filled.T


def conv_silu(p, taps, masks):
    summed = p * taps[3:4, :]
    for offset in range(1, 4):
        shifted = pltpu.roll(p, offset, 0)
        summed = summed + shifted * masks[offset - 1] * taps[3 - offset : 4 - offset, :]
    return silu(summed)


def unit(x):
    return x * lax.rsqrt(jnp.sum(x * x, axis=-1, keepdims=True) + 1e-06)


def mix_kernel(
    rate_ref, bias_ref, x0_ref, x1_ref, x2_ref, x3_ref, near_ref, far_ref, other_near_ref, other_far_ref, last_ref,
    seg_ref, tq_ref, tk_ref, tv_ref, gain_ref, out_ref, x_ref, w_ref, p_ref
):
    rows = p_ref.shape[0]
    quarter = rows // 4
    mine = lax.axis_index("tp") // 4
    for ref, behind in ((x0_ref, 0), (x1_ref, 1), (x2_ref, 2), (x3_ref, 3)):
        place = lax.rem(mine + 4 - behind, 4)
        x_ref[pl.ds(pl.multiple_of(place * quarter, quarter), quarter), :] = ref[...]
    group = lax.axis_index("dp")
    line = group // 2
    sign = 2 * lax.rem(group, 2) - 1
    for ref, offsets, way in (
        (near_ref, NEAR, sign), (far_ref, FAR, sign), (other_near_ref, NEAR, -sign), (other_far_ref, FAR, -sign), (last_ref, (8,), sign)
    ):
        for at, offset in enumerate(offsets):
            if ref is other_near_ref and offset == 0:
                continue
            place = lax.rem(line + 16 + way * offset, 16)
            w_ref[pl.ds(pl.multiple_of(place * 128, 128), 128), :] = ref[at * 128 : (at + 1) * 128, :]
    p_ref[...] = jnp.dot(x_ref[...], w_ref[...], preferred_element_type=jnp.float32).astype(jnp.bfloat16)
    blocks = rows // BLOCK
    seg_row = seg_ref[...].astype(jnp.float32)
    position = iota((1, rows), 1)
    masks = []
    for offset in range(1, 4):
        earlier = pltpu.roll(jnp.broadcast_to(seg_row, (8, rows)), offset, 1)[0:1]
        masks.append(jnp.where((position >= offset) & (earlier == seg_row), 1.0, 0.0))

    ba = p_ref[:, 768:896].astype(jnp.float32).T
    beta = 1.0 / (1.0 + jnp.exp(-ba[0:2]))
    rate = jnp.where(iota((2, 1), 0) == 0, rate_ref[0], rate_ref[1])
    bias = jnp.where(iota((2, 1), 0) == 0, bias_ref[0], bias_ref[1])
    decay = -rate * softplus(ba[2:4] + bias)
    upper = (iota((BLOCK, BLOCK), 0) <= iota((BLOCK, BLOCK), 1)).astype(jnp.bfloat16)
    decay_wide = jnp.concatenate([decay, jnp.zeros((6, rows), jnp.float32)], axis=0)
    stacked = jnp.concatenate(
        [decay_wide[:, b * BLOCK : (b + 1) * BLOCK] for b in range(blocks)], axis=0
    )
    high, low = split_two(stacked)
    lowest = (stacked - high.astype(jnp.float32) - low.astype(jnp.float32)).astype(jnp.bfloat16)
    total = jnp.dot(
        jnp.concatenate([high, low, lowest], axis=1),
        jnp.concatenate([upper, upper, upper], axis=0),
        preferred_element_type=jnp.float32,
    )
    cumulative, start, tail = [], [], []
    for b in range(blocks):
        part = total[8 * b : 8 * b + 2]
        seg_part = seg_row[:, b * BLOCK : (b + 1) * BLOCK]
        if b == 0:
            carried = jnp.zeros((1, BLOCK), jnp.float32)
        else:
            carried = jnp.where(seg_part == seg_row[:, b * BLOCK - 1 : b * BLOCK], 1.0, 0.0)
        closing = jnp.where(seg_part == seg_part[:, BLOCK - 1 :], 1.0, 0.0)
        cumulative.append(part)
        start.append(jnp.exp(part) * carried)
        tail.append(jnp.exp(part[:, BLOCK - 1 :] - part) * closing)
    cumulative = jnp.concatenate(cumulative, axis=1)
    start = jnp.concatenate(start, axis=1)
    tail = jnp.concatenate(tail, axis=1)
    cols = columns_of(
        jnp.concatenate([beta, cumulative, start, tail, beta * start, seg_row] + masks, axis=0)
    )
    mask_cols = [cols[:, 11 + i : 12 + i] for i in range(3)]

    query = unit(conv_silu(p_ref[:, 0:128].astype(jnp.float32), tq_ref[...], mask_cols)) * 128 ** (-0.5)
    key = unit(conv_silu(p_ref[:, 128:256].astype(jnp.float32), tk_ref[...], mask_cols))
    values = [
        conv_silu(
            p_ref[:, 256 + 128 * h : 384 + 128 * h].astype(jnp.float32),
            tv_ref[:, 128 * h : 128 * (h + 1)],
            mask_cols,
        )
        for h in range(2)
    ]

    row_at = iota((BLOCK, BLOCK), 0)
    col_at = iota((BLOCK, BLOCK), 1)
    base_diagonal = (row_at // BASE) == (col_at // BASE)
    picks = jnp.concatenate(
        [((row_at // BASE == col_at // BASE) & (row_at % BASE == j)).astype(jnp.bfloat16) for j in range(BASE - 1)],
        axis=1,
    )
    picks = jnp.concatenate([picks, picks], axis=0)

    problems = [(b, h) for b in range(blocks) for h in range(2)]
    scores, lowers, packed = {}, {}, []
    for b in range(blocks):
        span = slice(b * BLOCK, (b + 1) * BLOCK)
        k_b = key[span]
        grams = dot_split(jnp.concatenate([k_b, query[span]], axis=0), k_b.T)
        same = cols[span, 10:11] == seg_row[:, span]
        for h in range(2):
            spread = jnp.where(row_at >= col_at, cols[span, 2 + h : 3 + h] - cumulative[h : h + 1, span], 0.0)
            matrix = jnp.where((row_at >= col_at) & same, jnp.exp(spread), 0.0)
            scores[b, h] = grams[BLOCK:] * matrix
            lowers[b, h] = jnp.where(
                row_at > col_at, cols[span, h : h + 1] * grams[:BLOCK] * matrix, 0.0
            )
            masked = jnp.where(base_diagonal, lowers[b, h], 0.0)
            slab = masked[0:BASE]
            for d in range(1, BLOCK // BASE):
                slab = slab + masked[d * BASE : (d + 1) * BASE]
            packed.append(slab)
    high, low = split_two(jnp.concatenate(packed, axis=0))
    spread_columns = jnp.dot(
        jnp.concatenate([high, low], axis=1), picks, preferred_element_type=jnp.float32
    )
    count = len(problems)
    unit_rows = (iota((count, BASE, BLOCK), 1) == iota((count, BASE, BLOCK), 2) % BASE).astype(jnp.float32)
    solved = unit_rows
    for j in range(BASE - 1):
        factor = spread_columns[:, j * BLOCK : (j + 1) * BLOCK].reshape(count, BASE, BLOCK)
        solved = solved - factor * solved[:, j : j + 1, :]

    inverses = {
        key_of: jnp.where(base_diagonal, jnp.concatenate([solved[i]] * (BLOCK // BASE), axis=0), 0.0)
        for i, key_of in enumerate(problems)
    }
    size = BASE
    while size < BLOCK:
        below = (row_at // (2 * size) == col_at // (2 * size)) & (row_at // size != col_at // size)
        left = {n: dot_split(inverses[n], jnp.where(below, lowers[n], 0.0)) for n in problems}
        inverses = {n: inverses[n] - dot_split(left[n], inverses[n]) for n in problems}
        size = 2 * size

    first, state = {}, {}
    for b, h in problems:
        span = slice(b * BLOCK, (b + 1) * BLOCK)
        right = jnp.concatenate(
            [cols[span, h : h + 1] * values[h][span], cols[span, 8 + h : 9 + h] * key[span]], axis=1
        )
        first[b, h] = dot_split(inverses[b, h], right)
    for b, h in problems:
        span = slice(b * BLOCK, (b + 1) * BLOCK)
        if b < blocks - 1:
            state[b + 1, h] = dot_split((cols[span, 6 + h : 7 + h] * key[span]).T, first[b, h][:, :128])
    gain = gain_ref[...]
    carried = {}
    for b, h in problems:
        span = slice(b * BLOCK, (b + 1) * BLOCK)
        if b > 0:
            carried[b, h] = dot_split(
                jnp.concatenate([first[b, h][:, 128:], cols[span, 4 + h : 5 + h] * query[span]], axis=0),
                state[b, h],
            )
    outs = {}
    for b, h in problems:
        update = first[b, h][:, :128]
        if b > 0:
            outs[b, h] = carried[b, h][BLOCK:] + dot_split(scores[b, h], update - carried[b, h][:BLOCK])
        else:
            outs[b, h] = dot_split(scores[b, h], update)
    for b, h in problems:
        span = slice(b * BLOCK, (b + 1) * BLOCK)
        mixed = outs[b, h]
        normed = mixed * lax.rsqrt(jnp.mean(mixed * mixed, axis=-1, keepdims=True) + 1e-06) * gain
        gate = silu(p_ref[span, 512 + 128 * h : 640 + 128 * h].astype(jnp.float32))
        out_ref[span, 128 * h : 128 * (h + 1)] = (normed * gate).astype(jnp.bfloat16)


def rms_rows(tokens, gain):
    floats = tokens.astype(jnp.float32)
    scaled = floats * lax.rsqrt(jnp.mean(floats * floats, axis=-1, keepdims=True) + 1e-06)
    return (scaled * gain).astype(jnp.bfloat16)


def shards(
    tokens,
    norm_gain,
    w_query,
    w_key,
    w_value,
    w_gate,
    w_beta,
    w_decay,
    conv_query,
    conv_key,
    conv_value,
    decay_rate,
    dt_bias,
    out_gain,
    seg_ids,
):
    joined = jnp.concatenate(
        [w_query, w_key, w_value, w_gate, w_beta, w_decay, jnp.zeros((w_beta.shape[0], 124), jnp.bfloat16)], axis=1
    )
    normed = rms_rows(tokens, norm_gain)

    def along_z(block, shift):
        up = [(2 * z, 2 * ((z + shift) % 16)) for z in range(16)]
        down = [(2 * z + 1, 2 * ((z - shift) % 16) + 1) for z in range(16)]
        return lax.ppermute(block, "dp", up + down)

    def to_other_core(block):
        return lax.ppermute(block, "dp", [(i, i ^ 1) for i in range(32)])

    def along_x(block, shift):
        return lax.ppermute(block, "tp", [(i, (i + 4 * shift) % 16) for i in range(16)])

    chips = [[2 * z, 2 * z + 1] for z in range(16)]
    lines = [[4 * x + y for y in range(4)] for x in range(4)]
    pair = lax.all_gather(joined, "dp", axis=0, tiled=True, axis_index_groups=chips)
    by_four = along_z(pair, 4)
    quarter = lax.all_gather(normed, "tp", axis=0, tiled=True, axis_index_groups=lines)
    pair, by_four, quarter = lax.optimization_barrier((pair, by_four, quarter))
    behind, ahead = along_x(quarter, 1), along_x(quarter, 3)
    two = jnp.concatenate([pair, by_four], axis=0)
    by_two = along_z(two, 2)
    near = jnp.concatenate([two, by_two], axis=0)
    far = along_z(near, 1)
    last = along_z(by_two[128:], 2)
    across = along_x(behind, 1)
    ahead, held = lax.optimization_barrier((ahead, near))
    other_near = to_other_core(held)
    far, last, across, other_near = lax.optimization_barrier((far, last, across, other_near))
    weights = [near, far, other_near, to_other_core(far), last]
    rows = [quarter, behind, across, ahead]
    vmem = pl.BlockSpec(memory_space=pltpu.VMEM)
    smem = pl.BlockSpec(memory_space=pltpu.SMEM)
    tiles = pl.pallas_call(
        mix_kernel,
        out_shape=jax.ShapeDtypeStruct((512, 256), jnp.bfloat16),
        in_specs=[smem, smem] + [vmem] * 14,
        out_specs=vmem,
        scratch_shapes=[
            pltpu.VMEM((512, 2048), jnp.bfloat16),
            pltpu.VMEM((2048, 896), jnp.bfloat16),
            pltpu.VMEM((512, 896), jnp.bfloat16),
        ],
        compiler_params=pltpu.CompilerParams(vmem_limit_bytes=40 * 1024 * 1024),
    )(decay_rate, dt_bias, *rows, *weights, seg_ids, conv_query, conv_key, conv_value, out_gain.reshape(1, 128))
    return lax.all_to_all(tiles, "tp", split_axis=0, concat_axis=1, tiled=True)


def solution(mesh):
    in_specs = (
        P(("dp", "tp"), None),
        P(),
        P("dp", "tp"),
        P("dp", "tp"),
        P("dp", "tp"),
        P("dp", "tp"),
        P("dp", "tp"),
        P("dp", "tp"),
        P(None, "tp"),
        P(None, "tp"),
        P(None, "tp"),
        P("tp"),
        P("tp"),
        P(),
        P("dp", None),
    )
    out_specs = P(("dp", "tp"), None)
    return jax.shard_map(shards, mesh=mesh, in_specs=in_specs, out_specs=out_specs, check_vma=False)
```

```python
import jax
import jax.numpy as jnp
from jax import lax
from jax.experimental import pallas as pl
from jax.experimental.pallas import tpu as pltpu
from jax.sharding import PartitionSpec as P

BLOCK = 128
BASE = 16
NEAR = (0, 4, 2, 6)
FAR = (1, 5, 3, 7)


def split_two(x):
    high = x.astype(jnp.bfloat16)
    low = (x - high.astype(jnp.float32)).astype(jnp.bfloat16)
    return high, low


def dot_split(a, b):
    ah, al = split_two(a)
    bh, bl = split_two(b)
    if b.shape[1] > 128:
        high = jnp.concatenate([bh, bh], axis=0)
        both = jnp.concatenate([ah, al], axis=1)
        return jnp.dot(both, high, preferred_element_type=jnp.float32) + jnp.dot(
            ah, bl, preferred_element_type=jnp.float32
        )
    halves = jnp.concatenate([bh, bl], axis=1)
    both = jnp.dot(
        jnp.concatenate([ah, al], axis=1),
        jnp.concatenate([halves, halves], axis=0),
        preferred_element_type=jnp.float32,
    )
    return both[:, : b.shape[1]] + both[:, b.shape[1] :]


def iota(shape, axis):
    return lax.broadcasted_iota(jnp.int32, shape, axis)


def silu(x):
    return x / (1.0 + jnp.exp(-x))


def softplus(x):
    return jnp.maximum(x, 0.0) + jnp.log1p(jnp.exp(-jnp.abs(x)))


def columns_of(rows):
    filled = jnp.concatenate(
        [rows, jnp.zeros((128 - rows.shape[0], rows.shape[1]), jnp.float32)], axis=0
    )
    return filled.T


def conv_silu(p, taps, masks):
    summed = p * taps[3:4, :]
    for offset in range(1, 4):
        shifted = pltpu.roll(p, offset, 0)
        summed = summed + shifted * masks[offset - 1] * taps[3 - offset : 4 - offset, :]
    return silu(summed)


def unit(x):
    return x * lax.rsqrt(jnp.sum(x * x, axis=-1, keepdims=True) + 1e-06)


def pack_kernel(
    tokens_hbm, norm_hbm, query_hbm, key_hbm, value_hbm, gate_hbm, beta_ref, decay_ref, joined_ref, normed_ref,
    tokens_ref, norm_ref, sems
):
    moves = (
        (tokens_hbm, tokens_ref),
        (norm_hbm, norm_ref),
        (query_hbm, joined_ref.at[:, 0:128]),
        (key_hbm, joined_ref.at[:, 128:256]),
        (value_hbm, joined_ref.at[:, 256:512]),
        (gate_hbm, joined_ref.at[:, 512:768]),
    )
    copies = [pltpu.make_async_copy(source, target, sems.at[i]) for i, (source, target) in enumerate(moves)]
    for copy in copies:
        copy.start()
    for copy in copies:
        copy.wait()
    narrow = jnp.concatenate([beta_ref[...], decay_ref[...]], axis=0).astype(jnp.float32)
    narrow = jnp.concatenate([narrow, jnp.zeros((4, 64), jnp.float32)], axis=1)
    narrow = jnp.concatenate([narrow, jnp.zeros((124, 128), jnp.float32)], axis=0).T
    joined_ref[:, 768:896] = narrow[:64].astype(jnp.bfloat16)
    floats = tokens_ref[...].astype(jnp.float32)
    scaled = floats * lax.rsqrt(jnp.mean(floats * floats, axis=-1, keepdims=True) + 1e-06)
    normed_ref[...] = (scaled * norm_ref[...]).astype(jnp.bfloat16)


def project_kernel(
    x0_ref, x1_ref, x2_ref, x3_ref, near_ref, far_ref, other_near_ref, last_ref, sum_ref, left_ref, x_ref, part_ref
):
    quarter = x0_ref.shape[0]
    mine = lax.axis_index("tp") // 4
    for ref, behind in ((x0_ref, 0), (x1_ref, 1), (x2_ref, 2), (x3_ref, 3)):
        place = lax.rem(mine + 4 - behind, 4)
        x_ref[pl.ds(pl.multiple_of(place * quarter, quarter), quarter), :] = ref[...]
    group = lax.axis_index("dp")
    line = group // 2
    sign = 2 * lax.rem(group, 2) - 1

    def columns(offset):
        place = lax.rem(line + 16 + offset, 16)
        return x_ref[:, pl.ds(pl.multiple_of(place * 128, 128), 128)]

    offsets = [sign * n for n in NEAR + FAR] + [-sign * n for n in NEAR[1:]] + [8]
    for at, offset in enumerate(offsets):
        part_ref[:, at * 128 : (at + 1) * 128] = columns(offset)
    for at, n in enumerate(FAR):
        left_ref[:, at * 128 : (at + 1) * 128] = columns(-sign * n)
    total = jnp.dot(part_ref[:, 0:512], near_ref[...], preferred_element_type=jnp.float32)
    total = total + jnp.dot(part_ref[:, 512:1024], far_ref[...], preferred_element_type=jnp.float32)
    rest = jnp.concatenate([other_near_ref[128:, :], last_ref[...]], axis=0)
    sum_ref[...] = total + jnp.dot(part_ref[:, 1024:1536], rest, preferred_element_type=jnp.float32)


def mix_kernel(
    rate_ref, bias_ref, sum_ref, left_ref, other_far_ref, seg_ref, tq_ref, tk_ref, tv_ref, gain_ref, out_ref, p_ref
):
    rows = p_ref.shape[0]
    p_ref[...] = (
        sum_ref[...] + jnp.dot(left_ref[...], other_far_ref[...], preferred_element_type=jnp.float32)
    ).astype(jnp.bfloat16)
    blocks = rows // BLOCK
    seg_row = seg_ref[...].astype(jnp.float32)
    position = iota((1, rows), 1)
    masks = []
    for offset in range(1, 4):
        earlier = pltpu.roll(jnp.broadcast_to(seg_row, (8, rows)), offset, 1)[0:1]
        masks.append(jnp.where((position >= offset) & (earlier == seg_row), 1.0, 0.0))

    ba = p_ref[:, 768:896].astype(jnp.float32).T
    beta = 1.0 / (1.0 + jnp.exp(-ba[0:2]))
    rate = jnp.where(iota((2, 1), 0) == 0, rate_ref[0], rate_ref[1])
    bias = jnp.where(iota((2, 1), 0) == 0, bias_ref[0], bias_ref[1])
    decay = -rate * softplus(ba[2:4] + bias)
    upper = (iota((BLOCK, BLOCK), 0) <= iota((BLOCK, BLOCK), 1)).astype(jnp.bfloat16)
    decay_wide = jnp.concatenate([decay, jnp.zeros((6, rows), jnp.float32)], axis=0)
    stacked = jnp.concatenate(
        [decay_wide[:, b * BLOCK : (b + 1) * BLOCK] for b in range(blocks)], axis=0
    )
    high, low = split_two(stacked)
    lowest = (stacked - high.astype(jnp.float32) - low.astype(jnp.float32)).astype(jnp.bfloat16)
    total = jnp.dot(
        jnp.concatenate([high, low, lowest], axis=1),
        jnp.concatenate([upper, upper, upper], axis=0),
        preferred_element_type=jnp.float32,
    )
    cumulative, start, tail = [], [], []
    for b in range(blocks):
        part = total[8 * b : 8 * b + 2]
        seg_part = seg_row[:, b * BLOCK : (b + 1) * BLOCK]
        if b == 0:
            carried = jnp.zeros((1, BLOCK), jnp.float32)
        else:
            carried = jnp.where(seg_part == seg_row[:, b * BLOCK - 1 : b * BLOCK], 1.0, 0.0)
        closing = jnp.where(seg_part == seg_part[:, BLOCK - 1 :], 1.0, 0.0)
        cumulative.append(part)
        start.append(jnp.exp(part) * carried)
        tail.append(jnp.exp(part[:, BLOCK - 1 :] - part) * closing)
    cumulative = jnp.concatenate(cumulative, axis=1)
    start = jnp.concatenate(start, axis=1)
    tail = jnp.concatenate(tail, axis=1)
    cols = columns_of(
        jnp.concatenate([beta, cumulative, start, tail, beta * start, seg_row] + masks, axis=0)
    )
    mask_cols = [cols[:, 11 + i : 12 + i] for i in range(3)]

    query = unit(conv_silu(p_ref[:, 0:128].astype(jnp.float32), tq_ref[...], mask_cols)) * 128 ** (-0.5)
    key = unit(conv_silu(p_ref[:, 128:256].astype(jnp.float32), tk_ref[...], mask_cols))
    values = [
        conv_silu(
            p_ref[:, 256 + 128 * h : 384 + 128 * h].astype(jnp.float32),
            tv_ref[:, 128 * h : 128 * (h + 1)],
            mask_cols,
        )
        for h in range(2)
    ]

    row_at = iota((BLOCK, BLOCK), 0)
    col_at = iota((BLOCK, BLOCK), 1)
    base_diagonal = (row_at // BASE) == (col_at // BASE)
    picks = jnp.concatenate(
        [((row_at // BASE == col_at // BASE) & (row_at % BASE == j)).astype(jnp.bfloat16) for j in range(BASE - 1)],
        axis=1,
    )
    picks = jnp.concatenate([picks, picks], axis=0)

    problems = [(b, h) for b in range(blocks) for h in range(2)]
    scores, lowers, packed = {}, {}, []
    for b in range(blocks):
        span = slice(b * BLOCK, (b + 1) * BLOCK)
        k_b = key[span]
        grams = dot_split(jnp.concatenate([k_b, query[span]], axis=0), k_b.T)
        same = cols[span, 10:11] == seg_row[:, span]
        for h in range(2):
            spread = jnp.where(row_at >= col_at, cols[span, 2 + h : 3 + h] - cumulative[h : h + 1, span], 0.0)
            matrix = jnp.where((row_at >= col_at) & same, jnp.exp(spread), 0.0)
            scores[b, h] = grams[BLOCK:] * matrix
            lowers[b, h] = jnp.where(
                row_at > col_at, cols[span, h : h + 1] * grams[:BLOCK] * matrix, 0.0
            )
            masked = jnp.where(base_diagonal, lowers[b, h], 0.0)
            slab = masked[0:BASE]
            for d in range(1, BLOCK // BASE):
                slab = slab + masked[d * BASE : (d + 1) * BASE]
            packed.append(slab)
    high, low = split_two(jnp.concatenate(packed, axis=0))
    spread_columns = jnp.dot(
        jnp.concatenate([high, low], axis=1), picks, preferred_element_type=jnp.float32
    )
    count = len(problems)
    unit_rows = (iota((count, BASE, BLOCK), 1) == iota((count, BASE, BLOCK), 2) % BASE).astype(jnp.float32)
    solved = unit_rows
    for j in range(BASE - 1):
        factor = spread_columns[:, j * BLOCK : (j + 1) * BLOCK].reshape(count, BASE, BLOCK)
        solved = solved - factor * solved[:, j : j + 1, :]

    inverses = {
        key_of: jnp.where(base_diagonal, jnp.concatenate([solved[i]] * (BLOCK // BASE), axis=0), 0.0)
        for i, key_of in enumerate(problems)
    }
    size = BASE
    while size < BLOCK:
        below = (row_at // (2 * size) == col_at // (2 * size)) & (row_at // size != col_at // size)
        left = {n: dot_split(inverses[n], jnp.where(below, lowers[n], 0.0)) for n in problems}
        inverses = {n: inverses[n] - dot_split(left[n], inverses[n]) for n in problems}
        size = 2 * size

    first, state = {}, {}
    for b, h in problems:
        span = slice(b * BLOCK, (b + 1) * BLOCK)
        right = jnp.concatenate(
            [cols[span, h : h + 1] * values[h][span], cols[span, 8 + h : 9 + h] * key[span]], axis=1
        )
        first[b, h] = dot_split(inverses[b, h], right)
    for b, h in problems:
        span = slice(b * BLOCK, (b + 1) * BLOCK)
        if b < blocks - 1:
            state[b + 1, h] = dot_split((cols[span, 6 + h : 7 + h] * key[span]).T, first[b, h][:, :128])
    gain = gain_ref[...]
    carried = {}
    for b, h in problems:
        span = slice(b * BLOCK, (b + 1) * BLOCK)
        if b > 0:
            carried[b, h] = dot_split(
                jnp.concatenate([first[b, h][:, 128:], cols[span, 4 + h : 5 + h] * query[span]], axis=0),
                state[b, h],
            )
    outs = {}
    for b, h in problems:
        update = first[b, h][:, :128]
        if b > 0:
            outs[b, h] = carried[b, h][BLOCK:] + dot_split(scores[b, h], update - carried[b, h][:BLOCK])
        else:
            outs[b, h] = dot_split(scores[b, h], update)
    for b, h in problems:
        span = slice(b * BLOCK, (b + 1) * BLOCK)
        mixed = outs[b, h]
        normed = mixed * lax.rsqrt(jnp.mean(mixed * mixed, axis=-1, keepdims=True) + 1e-06) * gain
        gate = silu(p_ref[span, 512 + 128 * h : 640 + 128 * h].astype(jnp.float32))
        out_ref[span, 128 * h : 128 * (h + 1)] = (normed * gate).astype(jnp.bfloat16)


def shards(
    tokens,
    norm_gain,
    w_query,
    w_key,
    w_value,
    w_gate,
    w_beta,
    w_decay,
    conv_query,
    conv_key,
    conv_value,
    decay_rate,
    dt_bias,
    out_gain,
    seg_ids,
):
    vmem = pl.BlockSpec(memory_space=pltpu.VMEM)
    smem = pl.BlockSpec(memory_space=pltpu.SMEM)
    params = pltpu.CompilerParams(vmem_limit_bytes=40 * 1024 * 1024)
    joined, normed = pl.pallas_call(
        pack_kernel,
        out_shape=(
            jax.ShapeDtypeStruct((64, 896), jnp.bfloat16),
            jax.ShapeDtypeStruct(tokens.shape, jnp.bfloat16),
        ),
        in_specs=[pl.BlockSpec(memory_space=pl.ANY)] * 6 + [vmem] * 2,
        out_specs=(vmem, vmem),
        scratch_shapes=[
            pltpu.VMEM(tokens.shape, jnp.bfloat16),
            pltpu.VMEM((1, tokens.shape[1]), jnp.float32),
            pltpu.SemaphoreType.DMA((6,)),
        ],
        compiler_params=pltpu.CompilerParams(vmem_limit_bytes=58 * 1024 * 1024),
    )(tokens, norm_gain.reshape(1, -1), w_query, w_key, w_value, w_gate, w_beta.T, w_decay.T)

    def along_z(block, shift):
        up = [(2 * z, 2 * ((z + shift) % 16)) for z in range(16)]
        down = [(2 * z + 1, 2 * ((z - shift) % 16) + 1) for z in range(16)]
        return lax.ppermute(block, "dp", up + down)

    def to_other_core(block):
        return lax.ppermute(block, "dp", [(i, i ^ 1) for i in range(32)])

    def along_x(block, shift):
        return lax.ppermute(block, "tp", [(i, (i + 4 * shift) % 16) for i in range(16)])

    chips = [[2 * z, 2 * z + 1] for z in range(16)]
    lines = [[4 * x + y for y in range(4)] for x in range(4)]
    pair = lax.all_gather(joined, "dp", axis=0, tiled=True, axis_index_groups=chips)
    by_four = along_z(pair, 4)
    quarter = lax.all_gather(normed, "tp", axis=0, tiled=True, axis_index_groups=lines)
    pair, by_four, quarter = lax.optimization_barrier((pair, by_four, quarter))
    behind, ahead = along_x(quarter, 1), along_x(quarter, 3)
    two = jnp.concatenate([pair, by_four], axis=0)
    by_two = along_z(two, 2)
    near = jnp.concatenate([two, by_two], axis=0)
    far = along_z(near, 1)
    last = along_z(by_two[128:], 2)
    across = along_x(ahead, 3)
    behind, held = lax.optimization_barrier((behind, near))
    other_near = to_other_core(held)
    far, last, across, other_near = lax.optimization_barrier((far, last, across, other_near))
    other_far = to_other_core(far)
    partial, left = pl.pallas_call(
        project_kernel,
        out_shape=(
            jax.ShapeDtypeStruct((512, 896), jnp.float32),
            jax.ShapeDtypeStruct((512, 512), jnp.bfloat16),
        ),
        in_specs=[vmem] * 8,
        out_specs=(vmem, vmem),
        scratch_shapes=[pltpu.VMEM((512, 2048), jnp.bfloat16), pltpu.VMEM((512, 1536), jnp.bfloat16)],
        compiler_params=params,
        cost_estimate=pl.CostEstimate(flops=2 * 512 * 1536 * 896, bytes_accessed=8 << 20, transcendentals=0),
    )(quarter, behind, across, ahead, near, far, other_near, last)
    tiles = pl.pallas_call(
        mix_kernel,
        out_shape=jax.ShapeDtypeStruct((512, 256), jnp.bfloat16),
        in_specs=[smem, smem] + [vmem] * 8,
        out_specs=vmem,
        scratch_shapes=[pltpu.VMEM((512, 896), jnp.bfloat16)],
        compiler_params=params,
    )(decay_rate, dt_bias, partial, left, other_far, seg_ids, conv_query, conv_key, conv_value, out_gain.reshape(1, 128))
    return lax.all_to_all(tiles, "tp", split_axis=0, concat_axis=1, tiled=True)


def solution(mesh):
    in_specs = (
        P(("dp", "tp"), None),
        P(),
        P("dp", "tp"),
        P("dp", "tp"),
        P("dp", "tp"),
        P("dp", "tp"),
        P("dp", "tp"),
        P("dp", "tp"),
        P(None, "tp"),
        P(None, "tp"),
        P(None, "tp"),
        P("tp"),
        P("tp"),
        P(),
        P("dp", None),
    )
    out_specs = P(("dp", "tp"), None)
    return jax.shard_map(shards, mesh=mesh, in_specs=in_specs, out_specs=out_specs, check_vma=False)
```

```python
import jax
import jax.numpy as jnp
from jax import lax
from jax.experimental import pallas as pl
from jax.experimental.pallas import tpu as pltpu
from jax.sharding import PartitionSpec as P

BLOCK = 128
BASE = 16
NEAR = (0, 4, 2, 6)
FAR = (1, 5, 3, 7)


def split_two(x):
    high = x.astype(jnp.bfloat16)
    low = (x - high.astype(jnp.float32)).astype(jnp.bfloat16)
    return high, low


def dot_split(a, b):
    ah, al = split_two(a)
    bh, bl = split_two(b)
    if b.shape[1] > 128:
        high = jnp.concatenate([bh, bh], axis=0)
        both = jnp.concatenate([ah, al], axis=1)
        return jnp.dot(both, high, preferred_element_type=jnp.float32) + jnp.dot(
            ah, bl, preferred_element_type=jnp.float32
        )
    halves = jnp.concatenate([bh, bl], axis=1)
    both = jnp.dot(
        jnp.concatenate([ah, al], axis=1),
        jnp.concatenate([halves, halves], axis=0),
        preferred_element_type=jnp.float32,
    )
    return both[:, : b.shape[1]] + both[:, b.shape[1] :]


def iota(shape, axis):
    return lax.broadcasted_iota(jnp.int32, shape, axis)


def silu(x):
    return x / (1.0 + jnp.exp(-x))


def softplus(x):
    return jnp.maximum(x, 0.0) + jnp.log1p(jnp.exp(-jnp.abs(x)))


def columns_of(rows):
    filled = jnp.concatenate(
        [rows, jnp.zeros((128 - rows.shape[0], rows.shape[1]), jnp.float32)], axis=0
    )
    return filled.T


def conv_silu(p, taps, masks):
    summed = p * taps[3:4, :]
    for offset in range(1, 4):
        shifted = pltpu.roll(p, offset, 0)
        summed = summed + shifted * masks[offset - 1] * taps[3 - offset : 4 - offset, :]
    return silu(summed)


def unit(x):
    return x * lax.rsqrt(jnp.sum(x * x, axis=-1, keepdims=True) + 1e-06)


def pack_kernel(
    tokens_hbm, norm_hbm, query_hbm, key_hbm, value_hbm, gate_hbm, beta_ref, decay_ref, joined_ref, normed_ref,
    tokens_ref, norm_ref, sems
):
    moves = (
        (tokens_hbm, tokens_ref),
        (norm_hbm, norm_ref),
        (query_hbm, joined_ref.at[:, 0:128]),
        (key_hbm, joined_ref.at[:, 128:256]),
        (value_hbm, joined_ref.at[:, 256:512]),
        (gate_hbm, joined_ref.at[:, 512:768]),
    )
    copies = [pltpu.make_async_copy(source, target, sems.at[i]) for i, (source, target) in enumerate(moves)]
    for copy in copies:
        copy.start()
    narrow = jnp.concatenate([beta_ref[...], decay_ref[...]], axis=0).astype(jnp.float32)
    narrow = jnp.concatenate([narrow, jnp.zeros((4, 64), jnp.float32)], axis=1)
    narrow = jnp.concatenate([narrow, jnp.zeros((124, 128), jnp.float32)], axis=0).T
    copies[0].wait()
    copies[1].wait()
    floats = tokens_ref[...].astype(jnp.float32)
    scaled = floats * lax.rsqrt(jnp.mean(floats * floats, axis=-1, keepdims=True) + 1e-06)
    normed_ref[...] = (scaled * norm_ref[...]).astype(jnp.bfloat16)
    for copy in copies[2:]:
        copy.wait()
    joined_ref[:, 768:896] = narrow[:64].astype(jnp.bfloat16)


def project_kernel(
    x0_ref, x1_ref, x2_ref, x3_ref, near_ref, far_ref, other_near_ref, last_ref, sum_ref, left_ref, x_ref, part_ref
):
    quarter = x0_ref.shape[0]
    mine = lax.axis_index("tp") // 4
    for ref, behind in ((x0_ref, 0), (x1_ref, 1), (x2_ref, 2), (x3_ref, 3)):
        place = lax.rem(mine + 4 - behind, 4)
        x_ref[pl.ds(pl.multiple_of(place * quarter, quarter), quarter), :] = ref[...]
    group = lax.axis_index("dp")
    line = group // 2
    sign = 2 * lax.rem(group, 2) - 1

    def columns(offset):
        place = lax.rem(line + 16 + offset, 16)
        return x_ref[:, pl.ds(pl.multiple_of(place * 128, 128), 128)]

    offsets = [sign * n for n in NEAR + FAR] + [-sign * n for n in NEAR[1:]] + [8]
    for at, offset in enumerate(offsets):
        part_ref[:, at * 128 : (at + 1) * 128] = columns(offset)
    for at, n in enumerate(FAR):
        left_ref[:, at * 128 : (at + 1) * 128] = columns(-sign * n)
    total = jnp.dot(part_ref[:, 0:512], near_ref[...], preferred_element_type=jnp.float32)
    total = total + jnp.dot(part_ref[:, 512:1024], far_ref[...], preferred_element_type=jnp.float32)
    rest = jnp.concatenate([other_near_ref[128:, :], last_ref[...]], axis=0)
    sum_ref[...] = total + jnp.dot(part_ref[:, 1024:1536], rest, preferred_element_type=jnp.float32)


def mix_kernel(
    rate_ref, bias_ref, sum_ref, left_ref, other_far_ref, seg_ref, tq_ref, tk_ref, tv_ref, gain_ref, out_ref, p_ref
):
    rows = p_ref.shape[0]
    p_ref[...] = (
        sum_ref[...] + jnp.dot(left_ref[...], other_far_ref[...], preferred_element_type=jnp.float32)
    ).astype(jnp.bfloat16)
    blocks = rows // BLOCK
    seg_row = seg_ref[...].astype(jnp.float32)
    position = iota((1, rows), 1)
    masks = []
    for offset in range(1, 4):
        earlier = pltpu.roll(jnp.broadcast_to(seg_row, (8, rows)), offset, 1)[0:1]
        masks.append(jnp.where((position >= offset) & (earlier == seg_row), 1.0, 0.0))

    ba = p_ref[:, 768:896].astype(jnp.float32).T
    beta = 1.0 / (1.0 + jnp.exp(-ba[0:2]))
    rate = jnp.where(iota((2, 1), 0) == 0, rate_ref[0], rate_ref[1])
    bias = jnp.where(iota((2, 1), 0) == 0, bias_ref[0], bias_ref[1])
    decay = -rate * softplus(ba[2:4] + bias)
    upper = (iota((BLOCK, BLOCK), 0) <= iota((BLOCK, BLOCK), 1)).astype(jnp.bfloat16)
    decay_wide = jnp.concatenate([decay, jnp.zeros((6, rows), jnp.float32)], axis=0)
    stacked = jnp.concatenate(
        [decay_wide[:, b * BLOCK : (b + 1) * BLOCK] for b in range(blocks)], axis=0
    )
    high, low = split_two(stacked)
    lowest = (stacked - high.astype(jnp.float32) - low.astype(jnp.float32)).astype(jnp.bfloat16)
    total = jnp.dot(
        jnp.concatenate([high, low, lowest], axis=1),
        jnp.concatenate([upper, upper, upper], axis=0),
        preferred_element_type=jnp.float32,
    )
    cumulative, start, tail = [], [], []
    for b in range(blocks):
        part = total[8 * b : 8 * b + 2]
        seg_part = seg_row[:, b * BLOCK : (b + 1) * BLOCK]
        if b == 0:
            carried = jnp.zeros((1, BLOCK), jnp.float32)
        else:
            carried = jnp.where(seg_part == seg_row[:, b * BLOCK - 1 : b * BLOCK], 1.0, 0.0)
        closing = jnp.where(seg_part == seg_part[:, BLOCK - 1 :], 1.0, 0.0)
        cumulative.append(part)
        start.append(jnp.exp(part) * carried)
        tail.append(jnp.exp(part[:, BLOCK - 1 :] - part) * closing)
    cumulative = jnp.concatenate(cumulative, axis=1)
    start = jnp.concatenate(start, axis=1)
    tail = jnp.concatenate(tail, axis=1)
    cols = columns_of(
        jnp.concatenate([beta, cumulative, start, tail, beta * start, seg_row] + masks, axis=0)
    )
    mask_cols = [cols[:, 11 + i : 12 + i] for i in range(3)]

    query = unit(conv_silu(p_ref[:, 0:128].astype(jnp.float32), tq_ref[...], mask_cols)) * 128 ** (-0.5)
    key = unit(conv_silu(p_ref[:, 128:256].astype(jnp.float32), tk_ref[...], mask_cols))
    values = [
        conv_silu(
            p_ref[:, 256 + 128 * h : 384 + 128 * h].astype(jnp.float32),
            tv_ref[:, 128 * h : 128 * (h + 1)],
            mask_cols,
        )
        for h in range(2)
    ]

    row_at = iota((BLOCK, BLOCK), 0)
    col_at = iota((BLOCK, BLOCK), 1)
    base_diagonal = (row_at // BASE) == (col_at // BASE)
    picks = jnp.concatenate(
        [((row_at // BASE == col_at // BASE) & (row_at % BASE == j)).astype(jnp.bfloat16) for j in range(BASE - 1)],
        axis=1,
    )
    picks = jnp.concatenate([picks, picks], axis=0)

    problems = [(b, h) for b in range(blocks) for h in range(2)]
    scores, lowers, packed = {}, {}, []
    for b in range(blocks):
        span = slice(b * BLOCK, (b + 1) * BLOCK)
        k_b = key[span]
        grams = dot_split(jnp.concatenate([k_b, query[span]], axis=0), k_b.T)
        same = cols[span, 10:11] == seg_row[:, span]
        for h in range(2):
            spread = jnp.where(row_at >= col_at, cols[span, 2 + h : 3 + h] - cumulative[h : h + 1, span], 0.0)
            matrix = jnp.where((row_at >= col_at) & same, jnp.exp(spread), 0.0)
            scores[b, h] = grams[BLOCK:] * matrix
            lowers[b, h] = jnp.where(
                row_at > col_at, cols[span, h : h + 1] * grams[:BLOCK] * matrix, 0.0
            )
            masked = jnp.where(base_diagonal, lowers[b, h], 0.0)
            slab = masked[0:BASE]
            for d in range(1, BLOCK // BASE):
                slab = slab + masked[d * BASE : (d + 1) * BASE]
            packed.append(slab)
    high, low = split_two(jnp.concatenate(packed, axis=0))
    spread_columns = jnp.dot(
        jnp.concatenate([high, low], axis=1), picks, preferred_element_type=jnp.float32
    )
    count = len(problems)
    unit_rows = (iota((count, BASE, BLOCK), 1) == iota((count, BASE, BLOCK), 2) % BASE).astype(jnp.float32)
    solved = unit_rows
    for j in range(BASE - 1):
        factor = spread_columns[:, j * BLOCK : (j + 1) * BLOCK].reshape(count, BASE, BLOCK)
        solved = solved - factor * solved[:, j : j + 1, :]

    inverses = {
        key_of: jnp.where(base_diagonal, jnp.concatenate([solved[i]] * (BLOCK // BASE), axis=0), 0.0)
        for i, key_of in enumerate(problems)
    }
    size = BASE
    while size < BLOCK:
        below = (row_at // (2 * size) == col_at // (2 * size)) & (row_at // size != col_at // size)
        left = {n: dot_split(inverses[n], jnp.where(below, lowers[n], 0.0)) for n in problems}
        inverses = {n: inverses[n] - dot_split(left[n], inverses[n]) for n in problems}
        size = 2 * size

    first, state = {}, {}
    for b, h in problems:
        span = slice(b * BLOCK, (b + 1) * BLOCK)
        right = jnp.concatenate(
            [cols[span, h : h + 1] * values[h][span], cols[span, 8 + h : 9 + h] * key[span]], axis=1
        )
        first[b, h] = dot_split(inverses[b, h], right)
    for b, h in problems:
        span = slice(b * BLOCK, (b + 1) * BLOCK)
        if b < blocks - 1:
            state[b + 1, h] = dot_split((cols[span, 6 + h : 7 + h] * key[span]).T, first[b, h][:, :128])
    gain = gain_ref[...]
    carried = {}
    for b, h in problems:
        span = slice(b * BLOCK, (b + 1) * BLOCK)
        if b > 0:
            carried[b, h] = dot_split(
                jnp.concatenate([first[b, h][:, 128:], cols[span, 4 + h : 5 + h] * query[span]], axis=0),
                state[b, h],
            )
    outs = {}
    for b, h in problems:
        update = first[b, h][:, :128]
        if b > 0:
            outs[b, h] = carried[b, h][BLOCK:] + dot_split(scores[b, h], update - carried[b, h][:BLOCK])
        else:
            outs[b, h] = dot_split(scores[b, h], update)
    for b, h in problems:
        span = slice(b * BLOCK, (b + 1) * BLOCK)
        mixed = outs[b, h]
        normed = mixed * lax.rsqrt(jnp.mean(mixed * mixed, axis=-1, keepdims=True) + 1e-06) * gain
        gate = silu(p_ref[span, 512 + 128 * h : 640 + 128 * h].astype(jnp.float32))
        out_ref[span, 128 * h : 128 * (h + 1)] = (normed * gate).astype(jnp.bfloat16)


def shards(
    tokens,
    norm_gain,
    w_query,
    w_key,
    w_value,
    w_gate,
    w_beta,
    w_decay,
    conv_query,
    conv_key,
    conv_value,
    decay_rate,
    dt_bias,
    out_gain,
    seg_ids,
):
    vmem = pl.BlockSpec(memory_space=pltpu.VMEM)
    smem = pl.BlockSpec(memory_space=pltpu.SMEM)
    params = pltpu.CompilerParams(vmem_limit_bytes=40 * 1024 * 1024)
    joined, normed = pl.pallas_call(
        pack_kernel,
        out_shape=(
            jax.ShapeDtypeStruct((64, 896), jnp.bfloat16),
            jax.ShapeDtypeStruct(tokens.shape, jnp.bfloat16),
        ),
        in_specs=[pl.BlockSpec(memory_space=pl.ANY)] * 6 + [vmem] * 2,
        out_specs=(vmem, vmem),
        scratch_shapes=[
            pltpu.VMEM(tokens.shape, jnp.bfloat16),
            pltpu.VMEM((1, tokens.shape[1]), jnp.float32),
            pltpu.SemaphoreType.DMA((6,)),
        ],
        compiler_params=pltpu.CompilerParams(vmem_limit_bytes=58 * 1024 * 1024),
    )(tokens, norm_gain.reshape(1, -1), w_query, w_key, w_value, w_gate, w_beta.T, w_decay.T)

    def along_z(block, shift):
        up = [(2 * z, 2 * ((z + shift) % 16)) for z in range(16)]
        down = [(2 * z + 1, 2 * ((z - shift) % 16) + 1) for z in range(16)]
        return lax.ppermute(block, "dp", up + down)

    def to_other_core(block):
        return lax.ppermute(block, "dp", [(i, i ^ 1) for i in range(32)])

    def along_x(block, shift):
        return lax.ppermute(block, "tp", [(i, (i + 4 * shift) % 16) for i in range(16)])

    chips = [[2 * z, 2 * z + 1] for z in range(16)]
    lines = [[4 * x + y for y in range(4)] for x in range(4)]
    pair = lax.all_gather(joined, "dp", axis=0, tiled=True, axis_index_groups=chips)
    by_four = along_z(pair, 4)
    quarter = lax.all_gather(normed, "tp", axis=0, tiled=True, axis_index_groups=lines)
    pair, by_four, quarter = lax.optimization_barrier((pair, by_four, quarter))
    behind, ahead = along_x(quarter, 1), along_x(quarter, 3)
    two = jnp.concatenate([pair, by_four], axis=0)
    by_two = along_z(two, 2)
    near = jnp.concatenate([two, by_two], axis=0)
    far = along_z(near, 1)
    last = along_z(by_two[128:], 2)
    across = along_x(ahead, 3)
    behind, held = lax.optimization_barrier((behind, near))
    other_near = to_other_core(held)
    far, last, across, other_near = lax.optimization_barrier((far, last, across, other_near))
    other_far = to_other_core(far)
    partial, left = pl.pallas_call(
        project_kernel,
        out_shape=(
            jax.ShapeDtypeStruct((512, 896), jnp.float32),
            jax.ShapeDtypeStruct((512, 512), jnp.bfloat16),
        ),
        in_specs=[vmem] * 8,
        out_specs=(vmem, vmem),
        scratch_shapes=[pltpu.VMEM((512, 2048), jnp.bfloat16), pltpu.VMEM((512, 1536), jnp.bfloat16)],
        compiler_params=params,
        cost_estimate=pl.CostEstimate(flops=2 * 512 * 1536 * 896, bytes_accessed=8 << 20, transcendentals=0),
    )(quarter, behind, across, ahead, near, far, other_near, last)
    tiles = pl.pallas_call(
        mix_kernel,
        out_shape=jax.ShapeDtypeStruct((512, 256), jnp.bfloat16),
        in_specs=[smem, smem] + [vmem] * 8,
        out_specs=vmem,
        scratch_shapes=[pltpu.VMEM((512, 896), jnp.bfloat16)],
        compiler_params=params,
    )(decay_rate, dt_bias, partial, left, other_far, seg_ids, conv_query, conv_key, conv_value, out_gain.reshape(1, 128))
    return lax.all_to_all(tiles, "tp", split_axis=0, concat_axis=1, tiled=True)


def solution(mesh):
    in_specs = (
        P(("dp", "tp"), None),
        P(),
        P("dp", "tp"),
        P("dp", "tp"),
        P("dp", "tp"),
        P("dp", "tp"),
        P("dp", "tp"),
        P("dp", "tp"),
        P(None, "tp"),
        P(None, "tp"),
        P(None, "tp"),
        P("tp"),
        P("tp"),
        P(),
        P("dp", None),
    )
    out_specs = P(("dp", "tp"), None)
    return jax.shard_map(shards, mesh=mesh, in_specs=in_specs, out_specs=out_specs, check_vma=False)
```

```python
import jax
import jax.numpy as jnp
from jax import lax
from jax.experimental import pallas as pl
from jax.experimental.pallas import tpu as pltpu
from jax.sharding import PartitionSpec as P

BLOCK = 128
BASE = 16
NEAR = (0, 4, 2, 6)
FAR = (1, 5, 3, 7)


def split_two(x):
    high = x.astype(jnp.bfloat16)
    low = (x - high.astype(jnp.float32)).astype(jnp.bfloat16)
    return high, low


def dot_split(a, b):
    ah, al = split_two(a)
    bh, bl = split_two(b)
    if b.shape[1] > 128:
        high = jnp.concatenate([bh, bh], axis=0)
        both = jnp.concatenate([ah, al], axis=1)
        return jnp.dot(both, high, preferred_element_type=jnp.float32) + jnp.dot(
            ah, bl, preferred_element_type=jnp.float32
        )
    halves = jnp.concatenate([bh, bl], axis=1)
    both = jnp.dot(
        jnp.concatenate([ah, al], axis=1),
        jnp.concatenate([halves, halves], axis=0),
        preferred_element_type=jnp.float32,
    )
    return both[:, : b.shape[1]] + both[:, b.shape[1] :]


def iota(shape, axis):
    return lax.broadcasted_iota(jnp.int32, shape, axis)


def silu(x):
    return x / (1.0 + jnp.exp(-x))


def softplus(x):
    return jnp.maximum(x, 0.0) + jnp.log1p(jnp.exp(-jnp.abs(x)))


def columns_of(rows):
    filled = jnp.concatenate(
        [rows, jnp.zeros((128 - rows.shape[0], rows.shape[1]), jnp.float32)], axis=0
    )
    return filled.T


def conv_silu(p, taps, masks):
    summed = p * taps[3:4, :]
    for offset in range(1, 4):
        shifted = pltpu.roll(p, offset, 0)
        summed = summed + shifted * masks[offset - 1] * taps[3 - offset : 4 - offset, :]
    return silu(summed)


def unit(x):
    return x * lax.rsqrt(jnp.sum(x * x, axis=-1, keepdims=True) + 1e-06)


def pack_kernel(
    tokens_ref, norm_ref, query_ref, key_ref, value_ref, gate_ref, beta_ref, decay_ref, joined_ref, normed_ref
):
    joined_ref[:, 0:128] = query_ref[...]
    joined_ref[:, 128:256] = key_ref[...]
    joined_ref[:, 256:512] = value_ref[...]
    joined_ref[:, 512:768] = gate_ref[...]
    narrow = jnp.concatenate([beta_ref[...], decay_ref[...]], axis=0).astype(jnp.float32)
    narrow = jnp.concatenate([narrow, jnp.zeros((4, 64), jnp.float32)], axis=1)
    narrow = jnp.concatenate([narrow, jnp.zeros((124, 128), jnp.float32)], axis=0).T
    joined_ref[:, 768:896] = narrow[:64].astype(jnp.bfloat16)
    floats = tokens_ref[...].astype(jnp.float32)
    scaled = floats * lax.rsqrt(jnp.mean(floats * floats, axis=-1, keepdims=True) + 1e-06)
    normed_ref[...] = (scaled * norm_ref[...]).astype(jnp.bfloat16)


def project_kernel(
    x0_ref, x1_ref, x2_ref, x3_ref, near_ref, far_ref, other_near_ref, last_ref, sum_ref, left_ref, x_ref, part_ref
):
    quarter = x0_ref.shape[0]
    mine = lax.axis_index("tp") // 4
    for ref, behind in ((x0_ref, 0), (x1_ref, 1), (x2_ref, 2), (x3_ref, 3)):
        place = lax.rem(mine + 4 - behind, 4)
        x_ref[pl.ds(pl.multiple_of(place * quarter, quarter), quarter), :] = ref[...]
    group = lax.axis_index("dp")
    line = group // 2
    sign = 2 * lax.rem(group, 2) - 1

    def columns(offset):
        place = lax.rem(line + 16 + offset, 16)
        return x_ref[:, pl.ds(pl.multiple_of(place * 128, 128), 128)]

    offsets = [sign * n for n in NEAR + FAR] + [-sign * n for n in NEAR[1:]] + [8]
    for at, offset in enumerate(offsets):
        part_ref[:, at * 128 : (at + 1) * 128] = columns(offset)
    for at, n in enumerate(FAR):
        left_ref[:, at * 128 : (at + 1) * 128] = columns(-sign * n)
    total = jnp.dot(part_ref[:, 0:512], near_ref[...], preferred_element_type=jnp.float32)
    total = total + jnp.dot(part_ref[:, 512:1024], far_ref[...], preferred_element_type=jnp.float32)
    rest = jnp.concatenate([other_near_ref[128:, :], last_ref[...]], axis=0)
    sum_ref[...] = total + jnp.dot(part_ref[:, 1024:1536], rest, preferred_element_type=jnp.float32)


def mix_kernel(
    rate_ref, bias_ref, sum_ref, left_ref, other_far_ref, seg_ref, tq_ref, tk_ref, tv_ref, gain_ref, out_ref, p_ref
):
    rows = p_ref.shape[0]
    p_ref[...] = (
        sum_ref[...] + jnp.dot(left_ref[...], other_far_ref[...], preferred_element_type=jnp.float32)
    ).astype(jnp.bfloat16)
    blocks = rows // BLOCK
    seg_row = seg_ref[...].astype(jnp.float32)
    position = iota((1, rows), 1)
    masks = []
    for offset in range(1, 4):
        earlier = pltpu.roll(jnp.broadcast_to(seg_row, (8, rows)), offset, 1)[0:1]
        masks.append(jnp.where((position >= offset) & (earlier == seg_row), 1.0, 0.0))

    ba = p_ref[:, 768:896].astype(jnp.float32).T
    beta = 1.0 / (1.0 + jnp.exp(-ba[0:2]))
    rate = jnp.where(iota((2, 1), 0) == 0, rate_ref[0], rate_ref[1])
    bias = jnp.where(iota((2, 1), 0) == 0, bias_ref[0], bias_ref[1])
    decay = -rate * softplus(ba[2:4] + bias)
    upper = (iota((BLOCK, BLOCK), 0) <= iota((BLOCK, BLOCK), 1)).astype(jnp.bfloat16)
    decay_wide = jnp.concatenate([decay, jnp.zeros((6, rows), jnp.float32)], axis=0)
    stacked = jnp.concatenate(
        [decay_wide[:, b * BLOCK : (b + 1) * BLOCK] for b in range(blocks)], axis=0
    )
    high, low = split_two(stacked)
    lowest = (stacked - high.astype(jnp.float32) - low.astype(jnp.float32)).astype(jnp.bfloat16)
    total = jnp.dot(
        jnp.concatenate([high, low, lowest], axis=1),
        jnp.concatenate([upper, upper, upper], axis=0),
        preferred_element_type=jnp.float32,
    )
    cumulative, start, tail = [], [], []
    for b in range(blocks):
        part = total[8 * b : 8 * b + 2]
        seg_part = seg_row[:, b * BLOCK : (b + 1) * BLOCK]
        if b == 0:
            carried = jnp.zeros((1, BLOCK), jnp.float32)
        else:
            carried = jnp.where(seg_part == seg_row[:, b * BLOCK - 1 : b * BLOCK], 1.0, 0.0)
        closing = jnp.where(seg_part == seg_part[:, BLOCK - 1 :], 1.0, 0.0)
        cumulative.append(part)
        start.append(jnp.exp(part) * carried)
        tail.append(jnp.exp(part[:, BLOCK - 1 :] - part) * closing)
    cumulative = jnp.concatenate(cumulative, axis=1)
    start = jnp.concatenate(start, axis=1)
    tail = jnp.concatenate(tail, axis=1)
    cols = columns_of(
        jnp.concatenate([beta, cumulative, start, tail, beta * start, seg_row] + masks, axis=0)
    )
    mask_cols = [cols[:, 11 + i : 12 + i] for i in range(3)]

    query = unit(conv_silu(p_ref[:, 0:128].astype(jnp.float32), tq_ref[...], mask_cols)) * 128 ** (-0.5)
    key = unit(conv_silu(p_ref[:, 128:256].astype(jnp.float32), tk_ref[...], mask_cols))
    values = [
        conv_silu(
            p_ref[:, 256 + 128 * h : 384 + 128 * h].astype(jnp.float32),
            tv_ref[:, 128 * h : 128 * (h + 1)],
            mask_cols,
        )
        for h in range(2)
    ]

    row_at = iota((BLOCK, BLOCK), 0)
    col_at = iota((BLOCK, BLOCK), 1)
    base_diagonal = (row_at // BASE) == (col_at // BASE)
    picks = jnp.concatenate(
        [((row_at // BASE == col_at // BASE) & (row_at % BASE == j)).astype(jnp.bfloat16) for j in range(BASE - 1)],
        axis=1,
    )
    picks = jnp.concatenate([picks, picks], axis=0)

    problems = [(b, h) for b in range(blocks) for h in range(2)]
    scores, lowers, packed = {}, {}, []
    for b in range(blocks):
        span = slice(b * BLOCK, (b + 1) * BLOCK)
        k_b = key[span]
        grams = dot_split(jnp.concatenate([k_b, query[span]], axis=0), k_b.T)
        same = cols[span, 10:11] == seg_row[:, span]
        for h in range(2):
            spread = jnp.where(row_at >= col_at, cols[span, 2 + h : 3 + h] - cumulative[h : h + 1, span], 0.0)
            matrix = jnp.where((row_at >= col_at) & same, jnp.exp(spread), 0.0)
            scores[b, h] = grams[BLOCK:] * matrix
            lowers[b, h] = jnp.where(
                row_at > col_at, cols[span, h : h + 1] * grams[:BLOCK] * matrix, 0.0
            )
            masked = jnp.where(base_diagonal, lowers[b, h], 0.0)
            slab = masked[0:BASE]
            for d in range(1, BLOCK // BASE):
                slab = slab + masked[d * BASE : (d + 1) * BASE]
            packed.append(slab)
    high, low = split_two(jnp.concatenate(packed, axis=0))
    spread_columns = jnp.dot(
        jnp.concatenate([high, low], axis=1), picks, preferred_element_type=jnp.float32
    )
    count = len(problems)
    unit_rows = (iota((count, BASE, BLOCK), 1) == iota((count, BASE, BLOCK), 2) % BASE).astype(jnp.float32)
    solved = unit_rows
    for j in range(BASE - 1):
        factor = spread_columns[:, j * BLOCK : (j + 1) * BLOCK].reshape(count, BASE, BLOCK)
        solved = solved - factor * solved[:, j : j + 1, :]

    inverses = {
        key_of: jnp.where(base_diagonal, jnp.concatenate([solved[i]] * (BLOCK // BASE), axis=0), 0.0)
        for i, key_of in enumerate(problems)
    }
    size = BASE
    while size < BLOCK:
        below = (row_at // (2 * size) == col_at // (2 * size)) & (row_at // size != col_at // size)
        left = {n: dot_split(inverses[n], jnp.where(below, lowers[n], 0.0)) for n in problems}
        inverses = {n: inverses[n] - dot_split(left[n], inverses[n]) for n in problems}
        size = 2 * size

    first, state = {}, {}
    for b, h in problems:
        span = slice(b * BLOCK, (b + 1) * BLOCK)
        right = jnp.concatenate(
            [cols[span, h : h + 1] * values[h][span], cols[span, 8 + h : 9 + h] * key[span]], axis=1
        )
        first[b, h] = dot_split(inverses[b, h], right)
    for b, h in problems:
        span = slice(b * BLOCK, (b + 1) * BLOCK)
        if b < blocks - 1:
            state[b + 1, h] = dot_split((cols[span, 6 + h : 7 + h] * key[span]).T, first[b, h][:, :128])
    gain = gain_ref[...]
    carried = {}
    for b, h in problems:
        span = slice(b * BLOCK, (b + 1) * BLOCK)
        if b > 0:
            carried[b, h] = dot_split(
                jnp.concatenate([first[b, h][:, 128:], cols[span, 4 + h : 5 + h] * query[span]], axis=0),
                state[b, h],
            )
    outs = {}
    for b, h in problems:
        update = first[b, h][:, :128]
        if b > 0:
            outs[b, h] = carried[b, h][BLOCK:] + dot_split(scores[b, h], update - carried[b, h][:BLOCK])
        else:
            outs[b, h] = dot_split(scores[b, h], update)
    for b, h in problems:
        span = slice(b * BLOCK, (b + 1) * BLOCK)
        mixed = outs[b, h]
        normed = mixed * lax.rsqrt(jnp.mean(mixed * mixed, axis=-1, keepdims=True) + 1e-06) * gain
        gate = silu(p_ref[span, 512 + 128 * h : 640 + 128 * h].astype(jnp.float32))
        out_ref[span, 128 * h : 128 * (h + 1)] = (normed * gate).astype(jnp.bfloat16)


def shards(
    tokens,
    norm_gain,
    w_query,
    w_key,
    w_value,
    w_gate,
    w_beta,
    w_decay,
    conv_query,
    conv_key,
    conv_value,
    decay_rate,
    dt_bias,
    out_gain,
    seg_ids,
):
    vmem = pl.BlockSpec(memory_space=pltpu.VMEM)
    smem = pl.BlockSpec(memory_space=pltpu.SMEM)
    params = pltpu.CompilerParams(vmem_limit_bytes=40 * 1024 * 1024)
    joined, normed = pl.pallas_call(
        pack_kernel,
        out_shape=(
            jax.ShapeDtypeStruct((64, 896), jnp.bfloat16),
            jax.ShapeDtypeStruct(tokens.shape, jnp.bfloat16),
        ),
        in_specs=[vmem] * 8,
        out_specs=(vmem, vmem),
        compiler_params=pltpu.CompilerParams(vmem_limit_bytes=58 * 1024 * 1024),
    )(tokens, norm_gain.reshape(1, -1), w_query, w_key, w_value, w_gate, w_beta.T, w_decay.T)

    def along_z(block, shift):
        up = [(2 * z, 2 * ((z + shift) % 16)) for z in range(16)]
        down = [(2 * z + 1, 2 * ((z - shift) % 16) + 1) for z in range(16)]
        return lax.ppermute(block, "dp", up + down)

    def to_other_core(block):
        return lax.ppermute(block, "dp", [(i, i ^ 1) for i in range(32)])

    def along_x(block, shift):
        return lax.ppermute(block, "tp", [(i, (i + 4 * shift) % 16) for i in range(16)])

    chips = [[2 * z, 2 * z + 1] for z in range(16)]
    lines = [[4 * x + y for y in range(4)] for x in range(4)]
    pair = lax.all_gather(joined, "dp", axis=0, tiled=True, axis_index_groups=chips)
    by_four = along_z(pair, 4)
    quarter = lax.all_gather(normed, "tp", axis=0, tiled=True, axis_index_groups=lines)
    pair, by_four, quarter = lax.optimization_barrier((pair, by_four, quarter))
    behind, ahead = along_x(quarter, 1), along_x(quarter, 3)
    two = jnp.concatenate([pair, by_four], axis=0)
    by_two = along_z(two, 2)
    near = jnp.concatenate([two, by_two], axis=0)
    far = along_z(near, 1)
    last = along_z(by_two[128:], 2)
    across = along_x(ahead, 3)
    behind, held = lax.optimization_barrier((behind, near))
    other_near = to_other_core(held)
    far, last, across, other_near = lax.optimization_barrier((far, last, across, other_near))
    other_far = to_other_core(far)
    partial, left = pl.pallas_call(
        project_kernel,
        out_shape=(
            jax.ShapeDtypeStruct((512, 896), jnp.float32),
            jax.ShapeDtypeStruct((512, 512), jnp.bfloat16),
        ),
        in_specs=[vmem] * 8,
        out_specs=(vmem, vmem),
        scratch_shapes=[pltpu.VMEM((512, 2048), jnp.bfloat16), pltpu.VMEM((512, 1536), jnp.bfloat16)],
        compiler_params=params,
        cost_estimate=pl.CostEstimate(flops=2 * 512 * 1536 * 896, bytes_accessed=8 << 20, transcendentals=0),
    )(quarter, behind, across, ahead, near, far, other_near, last)
    tiles = pl.pallas_call(
        mix_kernel,
        out_shape=jax.ShapeDtypeStruct((512, 256), jnp.bfloat16),
        in_specs=[smem, smem] + [vmem] * 8,
        out_specs=vmem,
        scratch_shapes=[pltpu.VMEM((512, 896), jnp.bfloat16)],
        compiler_params=params,
    )(decay_rate, dt_bias, partial, left, other_far, seg_ids, conv_query, conv_key, conv_value, out_gain.reshape(1, 128))
    return lax.all_to_all(tiles, "tp", split_axis=0, concat_axis=1, tiled=True)


def solution(mesh):
    in_specs = (
        P(("dp", "tp"), None),
        P(),
        P("dp", "tp"),
        P("dp", "tp"),
        P("dp", "tp"),
        P("dp", "tp"),
        P("dp", "tp"),
        P("dp", "tp"),
        P(None, "tp"),
        P(None, "tp"),
        P(None, "tp"),
        P("tp"),
        P("tp"),
        P(),
        P("dp", None),
    )
    out_specs = P(("dp", "tp"), None)
    return jax.shard_map(shards, mesh=mesh, in_specs=in_specs, out_specs=out_specs, check_vma=False)
```
